512 devices in a mesh: leaf: 32 (over y, x), front: 16 (over z, core).
Axes of the slice: x: 4, y: 8, z: 8, core: 2. Of those that a mesh axis runs over, the one named last changes fastest.
Arguments:
- root_inverse: bfloat16 [384, 384], P('front')
- root_rhs: bfloat16 [384, 256], P('front'), may hold values from -6 to 6
- mid_panels: bfloat16 [4, 384, 384], P(None, 'front'), may hold values from -0.3125 to 0.3125
- mid_rows: int32 [4, 384], replicated, may hold values from 0 to 383, as said below
- mid_inverse: bfloat16 [4, 384, 384], P(None, 'front')
- mid_rhs: bfloat16 [4, 384, 256], P(None, 'front'), may hold values from -6 to 6
- parent_list: int32 [1024, 1], replicated, may hold values from 0 to 3
- sub_panels: bfloat16 [1024, 384, 384], P(('leaf', 'front')), may hold values from -0.3125 to 0.3125
- sub_rows: int32 [1024, 384], P(('leaf', 'front')), may hold values from 0 to 767, as said below
- sub_inverse: bfloat16 [1024, 384, 384], P(('leaf', 'front'))
- sub_rhs: bfloat16 [1024, 384, 256], P(('leaf', 'front')), may hold values from -6 to 6
- group_of: int32 [1024], P(('leaf', 'front')), may hold values from 0 to 1023, as said below
- leaf_panels: bfloat16 [1024, 384, 384], P(('leaf', 'front')), may hold values from -0.3125 to 0.3125
- leaf_rows: int32 [1024, 384], P(('leaf', 'front')), may hold values from 0 to 1151, as said below
- leaf_inverse: bfloat16 [1024, 384, 384], P(('leaf', 'front'))
- leaf_rhs: bfloat16 [1024, 384, 256], P(('leaf', 'front')), may hold values from -6 to 6
- live_cols: int32 [1024], P(('leaf', 'front')), may hold values from 192 to 384
Outputs:
- root_solution: bfloat16 [384, 256], P('front')
- mid_solution: bfloat16 [4, 384, 256], P(None, 'front')
- sub_solution: bfloat16 [1024, 384, 256], P(('leaf', 'front'))
- leaf_solution: bfloat16 [1024, 384, 256], P(('leaf', 'front'))
The draws below stay inside these ranges and needn't reach their ends.
Inputs may be any that keep to these rules, and one draw needn't show every extreme that they name: `mid_rows`: each row lists 384 different unknowns of the root. `sub_rows`: each row lists 384 different numbers; a < 384 names the root's unknown a, otherwise unknown a - 384 of the level-1 parent. `leaf_rows`: each row lists 384 different numbers; a < 384 names the root's unknown a, a < 768 unknown a - 384 of the level-1 grandparent, otherwise unknown a - 768 of the level-2 parent. `parent_list`: every level-1 supernode is the parent of some level-2 supernode. `group_of`: level-3 supernodes come in blocks of 2 and level-2 supernodes in blocks of 2, both numbered 0 to 511; the parent of a supernode of block d lies in a block whose cyclic distance from d is at most 2, and that distance is reached.
All inputs are finite; a program needn't handle non-finite values.
Results may differ from the reference program's by a relative error of at most 0.0067.
Values may be sent and summed in bfloat16 or wider, within the bound.
No kernel may reach another device: no remote copies, remote signals or barrier semaphores. Data moves between devices by JAX's collectives and lax.ppermute only.
A program may use at most 64 MiB of HBM per device.

```python
import math
import jax
import jax.numpy as jnp
from jax import lax

W = 384
R = 384
NRHS = 256
NMID = 4
HOP = 2
SUB_NODES = 2
LEAF_NODES = 2
SUBTREES = 1024
LEAVES = 1024
N_LEAF = 32
N_FRONT = 16


def triangle(diagonal, off_part):
    block_width = diagonal.shape[-1]
    lines = jnp.arange(block_width)
    upper = lines[:, None] < lines[None, :]
    same = lines[:, None] == lines[None, :]
    return jnp.where(same, diagonal[..., None], jnp.where(upper, off_part, 0.0))


def distinct_rows(key, count, span):
    keys = jax.random.split(key, count)
    return jax.vmap(lambda one_key: jax.random.permutation(one_key, span)[:R])(keys).astype(jnp.int32)


def inverse_blocks(key, count):
    first_key, second_key = jax.random.split(key)
    diagonal = jax.random.uniform(first_key, (count, W), minval=0.6, maxval=1.4)
    off_part = jax.random.normal(second_key, (count, W, W)) * (0.6 / math.sqrt(W))
    return triangle(diagonal, off_part).astype(jnp.bfloat16)


def draw_root_inverse(key, part):
    key = jax.random.fold_in(key, 31)
    return inverse_blocks(key, 1)[0]


def draw_mid_inverse(key, part):
    key = jax.random.fold_in(key, 32)
    return inverse_blocks(key, NMID)


def draw_sub_inverse(key, part):
    key = jax.random.fold_in(key, 33)
    return inverse_blocks(key, SUBTREES)


def draw_leaf_inverse(key, part):
    key = jax.random.fold_in(key, 34)
    return inverse_blocks(key, LEAVES)


def draw_mid_rows(key, part):
    key = jax.random.fold_in(key, 41)
    return distinct_rows(key, NMID, W)


def draw_sub_rows(key, part):
    key = jax.random.fold_in(key, 42)
    return distinct_rows(key, SUBTREES, 2 * W)


def draw_leaf_rows(key, part):
    key = jax.random.fold_in(key, 43)
    return distinct_rows(key, LEAVES, 3 * W)


def draw_group_of(key, part):
    key = jax.random.fold_in(key, 51)
    first_key, second_key, third_key, fourth_key = jax.random.split(key, 4)
    block_total = N_LEAF * N_FRONT
    numbers = jnp.arange(LEAVES, dtype=jnp.int32)
    block = numbers // LEAF_NODES
    offsets = jax.random.randint(first_key, (LEAVES,), -HOP, HOP + 1).astype(jnp.int32)
    upper_at = jax.random.randint(third_key, (), 0, LEAVES).astype(jnp.int32)
    lower_at = ((upper_at + 1 + jax.random.randint(fourth_key, (), 0, LEAVES - 1)) % LEAVES).astype(jnp.int32)
    offsets = jnp.where(numbers == upper_at, HOP, offsets)
    offsets = jnp.where(numbers == lower_at, -HOP, offsets)
    member = jax.random.randint(second_key, (LEAVES,), 0, SUB_NODES).astype(jnp.int32)
    return ((block + offsets + block_total) % block_total * SUB_NODES + member).astype(jnp.int32)


def place_ends(entries, rng, low, top_value):
    spot = [jax.random.randint(jax.random.fold_in(rng, axis), (), 0, length) for axis, length in enumerate(entries.shape)]
    main_axis = entries.shape.index(max(entries.shape))
    next_to = spot[:main_axis] + [(spot[main_axis] + 1) % entries.shape[main_axis]] + spot[main_axis + 1:]
    return entries.at[tuple(spot)].set(low).at[tuple(next_to)].set(top_value)


def shard_levels(own_key, extent, cuts, smallest, largest):
    level = 1.0
    for position, shards_of in cuts:
        draws = jax.random.uniform(jax.random.fold_in(jax.random.fold_in(own_key, 6), position), (shards_of,), jnp.float32, smallest / len(cuts), largest / len(cuts))
        level = level * jnp.repeat(jnp.exp(draws), extent[position] // shards_of).reshape((-1,) + (1,) * (len(extent) - 1 - position))
    return level


def distinct(own_key, rows, amount, top, lift):
    sequence = jax.random.permutation(jax.random.fold_in(own_key, 1), amount)
    favour = sequence
    for power in range(3):
        favour = favour * favour // amount
    favour = favour * lift // amount
    chance = jax.random.randint(jax.random.fold_in(own_key, 2), (rows, amount), 0, 4096) + favour
    fixed_rows = jax.random.permutation(jax.random.fold_in(own_key, 3), rows)[jnp.arange(amount) % rows]
    chance = jnp.where(jnp.arange(rows)[:, None] == fixed_rows[None, :], 1 << 14, chance)
    score = chance * amount + jnp.arange(amount)
    return lax.top_k(score.astype(jnp.int32), top)[1].astype(jnp.int32)


def bell_draw(key, extent, scale, bound, cuts=(), kind=jnp.bfloat16):
    values = scale * jax.random.normal(key, extent, jnp.float32)
    if cuts:
        values = values * shard_levels(key, extent, cuts, -0.22, 0.18)
    return jnp.clip(values, -bound, bound).astype(kind)


def setup_inputs(seed: int = 0) -> dict:
    key_list = jax.random.split(jax.random.key(seed), 18)
    return {
        "root_inverse": draw_root_inverse(jax.random.fold_in(key_list[17], 71), 0),
        "root_rhs": bell_draw(key_list[1], (W, NRHS), 1.0, 6.0, ((0, 16),)),
        "mid_panels": bell_draw(key_list[2], (NMID, R, W), R ** -0.5, 0.3125, ((1, 16),)),
        "mid_rows": draw_mid_rows(jax.random.fold_in(key_list[17], 71), 0),
        "mid_inverse": draw_mid_inverse(jax.random.fold_in(key_list[17], 71), 0),
        "mid_rhs": bell_draw(key_list[5], (NMID, W, NRHS), 1.0, 6.0, ((1, 16),)),
        "parent_list": distinct(key_list[6], SUBTREES, NMID, 1, 0),
        "sub_panels": bell_draw(key_list[7], (SUBTREES, R, W), R ** -0.5, 0.3125, ((0, 512),)),
        "sub_rows": draw_sub_rows(jax.random.fold_in(key_list[17], 71), 0),
        "sub_inverse": draw_sub_inverse(jax.random.fold_in(key_list[17], 71), 0),
        "sub_rhs": bell_draw(key_list[10], (SUBTREES, W, NRHS), 1.0, 6.0, ((0, 512),)),
        "group_of": draw_group_of(jax.random.fold_in(key_list[17], 71), 0),
        "leaf_panels": bell_draw(key_list[12], (LEAVES, R, W), R ** -0.5, 0.3125, ((0, 512),)),
        "leaf_rows": draw_leaf_rows(jax.random.fold_in(key_list[17], 71), 0),
        "leaf_inverse": draw_leaf_inverse(jax.random.fold_in(key_list[17], 71), 0),
        "leaf_rhs": bell_draw(key_list[15], (LEAVES, W, NRHS), 1.0, 6.0, ((0, 512),)),
        "live_cols": place_ends(jax.random.randint(key_list[16], (LEAVES,), W // 2, W + 1), jax.random.fold_in(key_list[16], 1), W // 2, W).astype(jnp.int32),
    }


def level_update(panels, picked, rhs):
    products = jnp.einsum("nrw,nrk->nwk", panels.astype(jnp.float32), picked.astype(jnp.float32))
    return (rhs.astype(jnp.float32) - products).astype(jnp.bfloat16)


def block_solve(inverse, update):
    return jnp.einsum("nji,nik->njk", inverse.astype(jnp.float32), update.astype(jnp.float32))


def pick_rows(known_rows, row_index):
    picked = jnp.take(known_rows, row_index.reshape(-1), axis=0)
    return picked.reshape(row_index.shape + (known_rows.shape[1],))


def in_blocks(array, count):
    return array.reshape((array.shape[0] // count, count) + array.shape[1:])


def reference(root_inverse, root_rhs, mid_panels, mid_rows, mid_inverse, mid_rhs, parent_list, sub_panels, sub_rows, sub_inverse, sub_rhs, group_of, leaf_panels, leaf_rows, leaf_inverse, leaf_rhs, live_cols):
    root_solution = jnp.dot(root_inverse, root_rhs, preferred_element_type=jnp.float32).astype(jnp.bfloat16)
    mid_gathered = pick_rows(root_solution, mid_rows)
    mid_solution = block_solve(mid_inverse, level_update(mid_panels, mid_gathered, mid_rhs)).astype(jnp.bfloat16)
    known_rows = jnp.concatenate([root_solution, mid_solution.reshape(-1, NRHS)], axis=0)
    parents = parent_list[:, 0]
    sub_index = jnp.where(sub_rows < W, sub_rows, parents[:, None] * W + sub_rows).astype(jnp.int32)

    def sub_block(pieces):
        panels, index, inverse, rhs = pieces
        picked = pick_rows(known_rows, index)
        return block_solve(inverse, level_update(panels, picked, rhs)).astype(jnp.bfloat16)

    sub_solution = lax.map(sub_block, (in_blocks(sub_panels, SUB_NODES), in_blocks(sub_index, SUB_NODES), in_blocks(sub_inverse, SUB_NODES), in_blocks(sub_rhs, SUB_NODES)))
    sub_solution = sub_solution.reshape(SUBTREES, W, NRHS)
    grandparent = parent_list[group_of, 0]
    all_known = jnp.concatenate([known_rows, sub_solution.reshape(-1, NRHS)], axis=0)
    leaf_index = jnp.where(leaf_rows < W, leaf_rows, jnp.where(leaf_rows < 2 * W, grandparent[:, None] * W + leaf_rows, (NMID - 1 + group_of[:, None]) * W + leaf_rows)).astype(jnp.int32)

    def leaf_block(pieces):
        panels, index, inverse, rhs, live = pieces
        picked = pick_rows(all_known, index)
        solved = block_solve(inverse, level_update(panels, picked, rhs))
        live_mask = jnp.arange(W, dtype=jnp.int32)[None, :] < live[:, None]
        return jnp.where(live_mask[:, :, None], solved, jnp.float32(0.0)).astype(jnp.bfloat16)

    leaf_solution = lax.map(leaf_block, (in_blocks(leaf_panels, LEAF_NODES), in_blocks(leaf_index, LEAF_NODES), in_blocks(leaf_inverse, LEAF_NODES), in_blocks(leaf_rhs, LEAF_NODES), in_blocks(live_cols, LEAF_NODES)))
    leaf_solution = leaf_solution.reshape(LEAVES, W, NRHS)
    return root_solution, mid_solution, sub_solution, leaf_solution
```

```python
import functools

import jax
import jax.numpy as jnp
from jax import lax
from jax.experimental import pallas as pl
from jax.experimental.pallas import tpu as pltpu
from jax.sharding import Mesh, PartitionSpec as P

HOP = 2
ALL = ("y", "x", "z", "c")
ROWS = ("z", "c")
W = 384
K = 256
HALF = W // 2
LANE = 128
BF16 = jnp.bfloat16
F32 = jnp.float32

VMEM = pl.BlockSpec(memory_space=pltpu.VMEM)
SMEM = pl.BlockSpec(memory_space=pltpu.SMEM)
ANY = pl.BlockSpec(memory_space=pl.ANY)


def shape(*dims, dtype=BF16):
    return jax.ShapeDtypeStruct(dims, dtype)


def call(body, outs, ins, macs, moved, scratch=()):
    return pl.pallas_call(
        body,
        out_shape=outs,
        in_specs=ins,
        out_specs=jax.tree.map(lambda _: VMEM, outs),
        scratch_shapes=scratch,
        cost_estimate=pl.CostEstimate(flops=2 * macs, bytes_accessed=moved, transcendentals=0),
        compiler_params=pltpu.CompilerParams(vmem_limit_bytes=40 * 2**20),
    )


def dot(a, b):
    return jnp.dot(a, b, preferred_element_type=F32)


def one_hot(index_row, first, blocks):
    spread = jnp.broadcast_to(index_row, (LANE, W)).T
    lane = lax.broadcasted_iota(jnp.int32, (W, LANE), 1) + first
    parts = [(spread == lane + LANE * j).astype(F32).astype(BF16) for j in range(blocks)]
    return jnp.concatenate(parts, axis=1)


def upper_kernel(got, mid_index, root, part):
    side = lax.rem(lax.axis_index("y"), 2)
    core = lax.axis_index("c")
    solved = dot(got[:, :W], got[:, W : W + K]).astype(BF16)
    root[...] = solved
    picked = dot(one_hot(mid_index[...], 0, W // LANE), solved).astype(BF16)
    products = dot(got[:, W + 2 * K + LANE :].T, picked)
    first = pl.multiple_of(side * HALF, 64)
    rhs = got[pl.ds(first, HALF), W + K : W + 2 * K].astype(F32)
    update = (rhs - products[:HALF]).astype(BF16)
    head = update[:LANE]
    tail = jnp.concatenate([jnp.zeros((LANE // 2, K), BF16), update[LANE:]], axis=0)
    rows = pl.ds(pl.multiple_of(core * HALF, 64), HALF)
    inverse_head = got[rows, W + 2 * K : W + 2 * K + LANE]
    inverse_tail = got[rows, W + 2 * K + 2 * LANE :]
    part[...] = (dot(inverse_head, head) + dot(inverse_tail, tail)).astype(BF16)


def sub_ready_kernel(rows, panels, rhs, root, base, spread):
    for n in range(2):
        index = rows[n : n + 1, :]
        turned = panels[n].T
        picked = dot(one_hot(index, 0, W // LANE), root[...]).astype(BF16)
        base[n] = rhs[n].astype(F32) - dot(turned, picked)
        spread[n] = dot(turned, one_hot(index, W, W // LANE)).astype(BF16)


def sub_kernel(parents, mid, base, spread, inverse, out):
    here = lax.axis_index(ALL)
    for n in range(2):
        parent = parents[2 * here + n]
        above = mid[pl.ds(pl.multiple_of(parent * W, W), W), :]
        update = (base[n] - dot(spread[n], above)).astype(BF16)
        out[n] = dot(inverse[n], update).astype(BF16)


def leaf_ready_kernel(parents, groups, rows, panels, rhs, root, mid, base, spread):
    for n in range(2):
        index = rows[n : n + 1, :]
        parent = parents[groups[n]]
        above = mid[pl.ds(pl.multiple_of(parent * W, W), W), :]
        turned = panels[n].T
        picked = dot(one_hot(index, 0, W // LANE), root[...])
        picked += dot(one_hot(index, W, W // LANE), above)
        base[n] = rhs[n].astype(F32) - dot(turned, picked.astype(BF16))
        spread[n] = dot(turned, one_hot(index, 2 * W, W // LANE)).astype(BF16)


def leaf_kernel(total, groups, live, base, spread, inverse, *rest):
    sources = rest[: 2 * HOP + 1]
    out, held, sems = rest[2 * HOP + 1 :]
    here = lax.axis_index(ALL)
    for n in range(2):
        group = groups[n]
        slot = lax.rem(group // 2 - here + total + HOP, total)
        member = lax.rem(group, 2)
        for j, source in enumerate(sources):

            @pl.when(slot == j)
            def _():
                pltpu.make_async_copy(source.at[member], held.at[n], sems.at[n]).start()

    for n in range(2):
        pltpu.make_async_copy(sources[0].at[0], held.at[n], sems.at[n]).wait()
        update = (base[n] - dot(spread[n], held[n])).astype(BF16)
        solved = dot(inverse[n], update)
        row = lax.broadcasted_iota(jnp.int32, (W, K), 0)
        out[n] = jnp.where(row < live[n], solved, 0.0).astype(BF16)


def per_device(
    root_inverse,
    root_rhs,
    mid_panels,
    mid_rows,
    mid_inverse,
    mid_rhs,
    parent_list,
    sub_panels,
    sub_rows,
    sub_inverse,
    sub_rhs,
    group_of,
    leaf_panels,
    leaf_rows,
    leaf_inverse,
    leaf_rhs,
    live_cols,
):
    node = lax.axis_index("x")
    side = lax.rem(lax.axis_index("y"), 2)
    own_rows = root_inverse.shape[0]
    total = lax.axis_size(ALL)
    parents = parent_list.reshape(-1)

    def pick_node(array):
        return lax.dynamic_index_in_dim(array, node, 0, keepdims=False)

    def pick_side(array):
        return jnp.where(side == 0, array[:, :HALF], array[:, HALF:])

    panel, inverse = pick_side(pick_node(mid_panels)), pick_side(pick_node(mid_inverse))
    packed = jnp.concatenate(
        [
            root_inverse,
            root_rhs,
            pick_node(mid_rhs),
            inverse[:, :LANE],
            panel,
            inverse[:, LANE:],
        ],
        axis=1,
    )
    got = lax.all_gather(packed, ROWS, axis=0, tiled=True)
    mid_index = lax.dynamic_slice_in_dim(mid_rows, node, 1, 0)
    root, part = call(
        upper_kernel,
        (shape(W, K), shape(HALF, K)),
        [VMEM, VMEM],
        2 * W * W * K,
        2 * W * 1280,
    )(got, mid_index)
    other = lax.ppermute(part, "y", [(i, i ^ 1) for i in range(lax.axis_size("y"))])
    base, spread = call(
        sub_ready_kernel,
        (shape(2, W, K, dtype=F32), shape(2, W, W)),
        [VMEM] * 4,
        8 * W * W * K,
        8 * W * W + 24 * W * K,
    )(sub_rows, sub_panels, sub_rhs, root)
    mid_half = (part.astype(F32) + other.astype(F32)).astype(BF16)
    mid_half, base, spread = lax.optimization_barrier((mid_half, base, spread))
    mid = lax.all_gather(mid_half, ("x", "c"), axis=0, tiled=True)
    sub_solution = call(
        sub_kernel,
        shape(2, W, K),
        [SMEM] + [VMEM] * 4,
        4 * W * W * K,
        12 * W * W + 16 * W * K,
    )(parents, mid, base, spread, sub_inverse)
    nearby = {0: sub_solution}
    for offset in (2, -2, 1, -1):
        route = [((i + offset) % total, i) for i in range(total)]
        nearby[offset] = lax.ppermute(sub_solution, ALL, route)
    leaf_base, leaf_spread = call(
        leaf_ready_kernel,
        (shape(2, W, K, dtype=F32), shape(2, W, W)),
        [SMEM, SMEM] + [VMEM] * 5,
        12 * W * W * K,
        8 * W * W + 24 * W * K,
    )(parents, group_of, leaf_rows, leaf_panels, leaf_rhs, root, mid)
    leaf_solution = call(
        functools.partial(leaf_kernel, total),
        shape(2, W, K),
        [SMEM, SMEM] + [VMEM] * 3 + [ANY] * (2 * HOP + 1),
        4 * W * W * K,
        12 * W * W + 24 * W * K,
        scratch=[pltpu.VMEM((2, W, K), BF16), pltpu.SemaphoreType.DMA((2,))],
    )(
        group_of,
        live_cols,
        leaf_base,
        leaf_spread,
        leaf_inverse,
        *(nearby[offset] for offset in range(-HOP, HOP + 1)),
    )
    first = lax.axis_index(ROWS) * own_rows
    root_own = lax.dynamic_slice_in_dim(root, first, own_rows, 0)
    mid_own = lax.dynamic_slice_in_dim(mid.reshape(-1, W, K), first, own_rows, 1)
    return (root_own, mid_own, sub_solution, leaf_solution)


def solution(mesh):
    chips = Mesh(mesh.devices.reshape(8, 4, 8, 2), ALL)
    lower = P(ALL, None, None)
    return jax.shard_map(
        per_device,
        mesh=chips,
        in_specs=(
            P(ROWS, None),
            P(ROWS, None),
            P(None, ROWS, None),
            P(),
            P(None, ROWS, None),
            P(None, ROWS, None),
            P(),
            lower,
            P(ALL, None),
            lower,
            lower,
            P(ALL),
            lower,
            P(ALL, None),
            lower,
            lower,
            P(ALL),
        ),
        out_specs=(P(ROWS, None), P(None, ROWS, None), lower, lower),
        check_vma=False,
    )
```

```python
import functools

import jax
import jax.numpy as jnp
from jax import lax
from jax.experimental import pallas as pl
from jax.experimental.pallas import tpu as pltpu
from jax.sharding import Mesh, PartitionSpec as P

HOP = 2
ALL = ("y", "x", "z", "c")
ROWS = ("z", "c")
W = 384
K = 256
HALF = W // 2
LANE = 128
BF16 = jnp.bfloat16
F32 = jnp.float32

VMEM = pl.BlockSpec(memory_space=pltpu.VMEM)
SMEM = pl.BlockSpec(memory_space=pltpu.SMEM)
ANY = pl.BlockSpec(memory_space=pl.ANY)
HBM = pl.BlockSpec(memory_space=pltpu.HBM)


def shape(*dims, dtype=BF16):
    return jax.ShapeDtypeStruct(dims, dtype)


def call(body, outs, ins, macs, moved, places=None, scratch=(), grant=16):
    return pl.pallas_call(
        body,
        out_shape=outs,
        in_specs=ins,
        out_specs=places or jax.tree.map(lambda _: VMEM, outs),
        scratch_shapes=scratch,
        cost_estimate=pl.CostEstimate(flops=2 * macs, bytes_accessed=moved, transcendentals=0),
        compiler_params=pltpu.CompilerParams(vmem_limit_bytes=int(grant * 2**20)),
    )


def dot(a, b):
    return jnp.dot(a, b, preferred_element_type=F32)


def one_hot(index_row, first, blocks):
    spread = jnp.broadcast_to(index_row, (LANE, W)).T
    lane = lax.broadcasted_iota(jnp.int32, (W, LANE), 1) + first
    parts = [(spread == lane + LANE * j).astype(F32).astype(BF16) for j in range(blocks)]
    return jnp.concatenate(parts, axis=1)


def pack_kernel(
    total,
    root_inverse,
    root_rhs,
    panels,
    inverses,
    rhs,
    parents_all,
    groups_all,
    live_all,
    out,
    facts,
    panel,
    inverse,
    parents,
    groups,
    live,
    sems,
):
    node = lax.axis_index("x")
    side = lax.rem(lax.axis_index("y"), 2)
    here = lax.axis_index(ALL)
    pairs = [
        (groups_all, groups),
        (parents_all, parents),
        (live_all, live),
        (panels.at[node], panel),
        (inverses.at[node], inverse),
        (root_inverse, out.at[:, :W]),
        (root_rhs, out.at[:, W : W + K]),
        (rhs.at[node], out.at[:, W + K : W + 2 * K]),
    ]
    copies = [pltpu.make_async_copy(a, b, sems.at[i]) for i, (a, b) in enumerate(pairs)]
    for copy in copies:
        copy.start()
    for copy in copies:
        copy.wait()
    values = []
    for n in range(2):
        group = groups[n]
        block = lax.rem(group // 2 - here + total + HOP, total) - HOP + lax.rem(here, 2)
        values += [parents[2 * here + n], parents[group], block, lax.rem(group, 2), live[n]]
    place = lax.broadcasted_iota(jnp.int32, facts.shape, 1)
    row = jnp.zeros(facts.shape, jnp.int32)
    for i, value in enumerate(values):
        row = jnp.where(place == i, value, row)
    facts[...] = row

    def half(array):
        return jnp.where(side == 0, array[:, :HALF], array[:, HALF:])

    inverse_half = half(inverse[...])
    out[:, W + 2 * K :] = jnp.concatenate(
        [inverse_half[:, :LANE], half(panel[...]), inverse_half[:, LANE:]], axis=1
    )


def upper_kernel(got, mid_rows, panels, inverses, root, part):
    del panels, inverses
    side = lax.rem(lax.axis_index("y"), 2)
    core = lax.axis_index("c")
    mid_index = mid_rows[pl.ds(lax.axis_index("x"), 1), :]
    solved = dot(got[:, :W], got[:, W : W + K]).astype(BF16)
    root[...] = solved
    picked = dot(one_hot(mid_index, 0, W // LANE), solved).astype(BF16)
    products = dot(got[:, W + 2 * K + LANE :].T, picked)
    first = pl.multiple_of(side * HALF, 64)
    rhs = got[pl.ds(first, HALF), W + K : W + 2 * K].astype(F32)
    update = (rhs - products[:HALF]).astype(BF16)
    head = update[:LANE]
    tail = jnp.concatenate([jnp.zeros((LANE // 2, K), BF16), update[LANE:]], axis=0)
    rows = pl.ds(pl.multiple_of(core * HALF, 64), HALF)
    inverse_head = got[rows, W + 2 * K : W + 2 * K + LANE]
    inverse_tail = got[rows, W + 2 * K + 2 * LANE :]
    part[...] = (dot(inverse_head, head) + dot(inverse_tail, tail)).astype(BF16)


def sub_ready_kernel(rows, panels, rhs, root, facts, base, spread):
    del facts
    for n in range(2):
        index = rows[n : n + 1, :]
        turned = panels[n].T
        picked = dot(one_hot(index, 0, W // LANE), root[...]).astype(BF16)
        base[n] = rhs[n].astype(F32) - dot(turned, picked)
        spread[n] = dot(turned, one_hot(index, W, W // LANE)).astype(BF16)


def rows_of(mid, parent):
    return mid[pl.ds(pl.multiple_of(parent * W, W), W), :]


def sub_kernel(facts, mid, base, spread, inverse, out):
    for n in range(2):
        update = (base[n] - dot(spread[n], rows_of(mid, facts[0, 5 * n]))).astype(BF16)
        out[n] = dot(inverse[n], update).astype(BF16)


def leaf_ready_kernel(
    facts, rows, panels, rhs, root, mid, solved, base, spread, root_own, mid_own, out, sem
):
    store = pltpu.make_async_copy(solved, out, sem)
    store.start()
    own_rows = root_own.shape[0]
    first = lax.axis_index(ROWS) * own_rows
    row = lax.broadcasted_iota(jnp.int32, (own_rows, W), 0) + first
    column = lax.broadcasted_iota(jnp.int32, (own_rows, W), 1)
    own = (row == column).astype(F32).astype(BF16)
    root_own[...] = dot(own, root[...]).astype(BF16)
    for s in range(mid_own.shape[0]):
        mid_own[s] = dot(own, mid[s * W : (s + 1) * W, :]).astype(BF16)
    for n in range(2):
        index = rows[n : n + 1, :]
        turned = panels[n].T
        picked = dot(one_hot(index, 0, W // LANE), root[...])
        picked += dot(one_hot(index, W, W // LANE), rows_of(mid, facts[0, 5 * n + 1]))
        base[n] = rhs[n].astype(F32) - dot(turned, picked.astype(BF16))
        spread[n] = dot(turned, one_hot(index, 2 * W, W // LANE)).astype(BF16)
    store.wait()


def leaf_kernel(facts, base, spread, inverse, chip, nearby, outer, out, held, done, sems):
    stores = []
    for n in range(2):
        block, member, live = (facts[0, 5 * n + i] for i in (2, 3, 4))

        @pl.when(jnp.logical_or(block == 0, block == 1))
        def _():
            held[n] = chip[2 * block + member]

        @pl.when(jnp.logical_or(block == -1, block == 2))
        def _():
            held[n] = nearby[jnp.where(block == 2, 0, 2) + member]

        @pl.when(jnp.logical_or(block == -2, block == 3))
        def _():
            held[n] = outer[member]

        update = (base[n] - dot(spread[n], held[n])).astype(BF16)
        solved = dot(inverse[n], update)
        row = lax.broadcasted_iota(jnp.int32, (W, K), 0)
        done[n] = jnp.where(row < live, solved, 0.0).astype(BF16)
        stores.append(pltpu.make_async_copy(done.at[n], out.at[n], sems.at[n]))
        stores[n].start()
    for store in stores:
        store.wait()


def per_device(
    root_inverse,
    root_rhs,
    mid_panels,
    mid_rows,
    mid_inverse,
    mid_rhs,
    parent_list,
    sub_panels,
    sub_rows,
    sub_inverse,
    sub_rhs,
    group_of,
    leaf_panels,
    leaf_rows,
    leaf_inverse,
    leaf_rhs,
    live_cols,
):
    own_rows = root_inverse.shape[0]
    total = lax.axis_size(ALL)
    parents = parent_list.reshape(-1)
    packed, facts = call(
        functools.partial(pack_kernel, total),
        (shape(own_rows, 1280), shape(1, LANE, dtype=jnp.int32)),
        [HBM] * 8,
        0,
        4 * own_rows * 1280,
        scratch=[pltpu.VMEM((own_rows, W), BF16)] * 2
        + [pltpu.SMEM(a.shape, jnp.int32) for a in (parents, group_of, live_cols)]
        + [pltpu.SemaphoreType.DMA((8,))],
        grant=60,
    )(root_inverse, root_rhs, mid_panels, mid_inverse, mid_rhs, parents, group_of, live_cols)
    got = lax.all_gather(packed, ROWS, axis=0, tiled=True)
    square, tall = shape(2, W, W), shape(2, W, K, dtype=F32)
    thin = shape(2, W, K)
    root, part = call(
        upper_kernel,
        (shape(W, K), shape(HALF, K)),
        [VMEM] * 4,
        2 * W * W * K,
        2 * W * 1280,
    )(got, mid_rows, leaf_panels, leaf_inverse)
    other = lax.ppermute(part, "y", [(i, i ^ 1) for i in range(lax.axis_size("y"))])
    base, spread = call(
        sub_ready_kernel,
        (tall, square),
        [VMEM] * 5,
        8 * W * W * K,
        8 * W * W + 24 * W * K,
    )(sub_rows, sub_panels, sub_rhs, root, facts)
    mid_half = (part.astype(F32) + other.astype(F32)).astype(BF16)
    mid_half, base = lax.optimization_barrier((mid_half, base))
    mid = lax.all_gather(mid_half, ("x", "c"), axis=0, tiled=True)
    solved = call(
        sub_kernel,
        shape(2, W, K),
        [SMEM] + [VMEM] * 4,
        4 * W * W * K,
        12 * W * W + 16 * W * K,
    )(facts, mid, base, spread, sub_inverse)
    chips = total // 2
    up = [((2 * m + 2 + c) % total, 2 * m + c) for m in range(chips) for c in range(2)]
    down = [((2 * m - 2 + c) % total, 2 * m + c) for m in range(chips) for c in range(2)]
    inner = lax.ppermute(solved, ALL, up[0::2] + down[1::2])
    outer = lax.ppermute(solved, ALL, down[0::2] + up[1::2])
    chip = lax.all_gather(solved, "c", axis=0, tiled=True)
    leaf_base, leaf_spread, root_own, mid_own, sub_solution = call(
        leaf_ready_kernel,
        (tall, square, shape(own_rows, K), shape(mid_rows.shape[0], own_rows, K), thin),
        [SMEM] + [VMEM] * 6,
        12 * W * W * K,
        8 * W * W + 24 * W * K,
        places=(VMEM,) * 4 + (HBM,),
        scratch=[pltpu.SemaphoreType.DMA],
    )(facts, leaf_rows, leaf_panels, leaf_rhs, root, mid, solved)
    inner, chip, leaf_base = lax.optimization_barrier((inner, chip, leaf_base))
    nearby = lax.all_gather(inner, "c", axis=0, tiled=True)
    leaf_solution = call(
        leaf_kernel,
        shape(2, W, K),
        [SMEM] + [VMEM] * 6,
        4 * W * W * K,
        12 * W * W + 24 * W * K,
        places=HBM,
        scratch=[pltpu.VMEM((2, W, K), BF16)] * 2 + [pltpu.SemaphoreType.DMA((2,))],
    )(facts, leaf_base, leaf_spread, leaf_inverse, chip, nearby, outer)
    return (root_own, mid_own, sub_solution, leaf_solution)


def solution(mesh):
    chips = Mesh(mesh.devices.reshape(8, 4, 8, 2), ALL)
    lower = P(ALL, None, None)
    return jax.shard_map(
        per_device,
        mesh=chips,
        in_specs=(
            P(ROWS, None),
            P(ROWS, None),
            P(None, ROWS, None),
            P(),
            P(None, ROWS, None),
            P(None, ROWS, None),
            P(),
            lower,
            P(ALL, None),
            lower,
            lower,
            P(ALL),
            lower,
            P(ALL, None),
            lower,
            lower,
            P(ALL),
        ),
        out_specs=(P(ROWS, None), P(None, ROWS, None), lower, lower),
        check_vma=False,
    )
```

```python
import functools

import jax
import jax.numpy as jnp
from jax import lax
from jax.experimental import pallas as pl
from jax.experimental.pallas import tpu as pltpu
from jax.sharding import Mesh, PartitionSpec as P

HOP = 2
ALL = ("y", "x", "z", "c")
ROWS = ("z", "c")
W = 384
K = 256
HALF = W // 2
LANE = 128
BF16 = jnp.bfloat16
F32 = jnp.float32

VMEM = pl.BlockSpec(memory_space=pltpu.VMEM)
SMEM = pl.BlockSpec(memory_space=pltpu.SMEM)
ANY = pl.BlockSpec(memory_space=pl.ANY)
HBM = pl.BlockSpec(memory_space=pltpu.HBM)


def shape(*dims, dtype=BF16):
    return jax.ShapeDtypeStruct(dims, dtype)


def call(body, outs, ins, macs, moved, places=None, scratch=(), grant=16):
    return pl.pallas_call(
        body,
        out_shape=outs,
        in_specs=ins,
        out_specs=places or jax.tree.map(lambda _: VMEM, outs),
        scratch_shapes=scratch,
        cost_estimate=pl.CostEstimate(flops=2 * macs, bytes_accessed=moved, transcendentals=0),
        compiler_params=pltpu.CompilerParams(vmem_limit_bytes=int(grant * 2**20)),
    )


def dot(a, b):
    return jnp.dot(a, b, preferred_element_type=F32)


def one_hot(index_row, first, blocks):
    spread = jnp.broadcast_to(index_row, (LANE, W)).T
    lane = lax.broadcasted_iota(jnp.int32, (W, LANE), 1) + first
    parts = [(spread == lane + LANE * j).astype(F32).astype(BF16) for j in range(blocks)]
    return jnp.concatenate(parts, axis=1)


def pack_kernel(
    total,
    root_inverse,
    root_rhs,
    panels,
    inverses,
    rhs,
    parents_all,
    groups_all,
    live_all,
    out,
    facts,
    panel,
    inverse,
    parents,
    groups,
    live,
    sems,
):
    node = lax.axis_index("x")
    side = lax.rem(lax.axis_index("y"), 2)
    here = lax.axis_index(ALL)
    pairs = [
        (groups_all, groups),
        (parents_all, parents),
        (live_all, live),
        (panels.at[node], panel),
        (inverses.at[node], inverse),
        (root_inverse, out.at[:, :W]),
        (root_rhs, out.at[:, W : W + K]),
        (rhs.at[node], out.at[:, W + K : W + 2 * K]),
    ]
    copies = [pltpu.make_async_copy(a, b, sems.at[i]) for i, (a, b) in enumerate(pairs)]
    for copy in copies:
        copy.start()
    for copy in copies:
        copy.wait()
    values = []
    for n in range(2):
        group = groups[n]
        block = lax.rem(group // 2 - here + total + HOP, total) - HOP + lax.rem(here, 2)
        values += [parents[2 * here + n], parents[group], block, lax.rem(group, 2), live[n]]
    place = lax.broadcasted_iota(jnp.int32, facts.shape, 1)
    row = jnp.zeros(facts.shape, jnp.int32)
    for i, value in enumerate(values):
        row = jnp.where(place == i, value, row)
    facts[...] = row

    def half(array):
        return jnp.where(side == 0, array[:, :HALF], array[:, HALF:])

    inverse_half = half(inverse[...])
    out[:, W + 2 * K :] = jnp.concatenate(
        [inverse_half[:, :LANE], half(panel[...]), inverse_half[:, LANE:]], axis=1
    )


def upper_kernel(got, mid_rows, panels, inverses, root, part):
    del panels, inverses
    side = lax.rem(lax.axis_index("y"), 2)
    core = lax.axis_index("c")
    mid_index = mid_rows[pl.ds(lax.axis_index("x"), 1), :]
    solved = dot(got[:, :W], got[:, W : W + K]).astype(BF16)
    root[...] = solved
    picked = dot(one_hot(mid_index, 0, W // LANE), solved).astype(BF16)
    products = dot(got[:, W + 2 * K + LANE :].T, picked)
    first = pl.multiple_of(side * HALF, 64)
    rhs = got[pl.ds(first, HALF), W + K : W + 2 * K].astype(F32)
    update = (rhs - products[:HALF]).astype(BF16)
    head = update[:LANE]
    tail = jnp.concatenate([jnp.zeros((LANE // 2, K), BF16), update[LANE:]], axis=0)
    rows = pl.ds(pl.multiple_of(core * HALF, 64), HALF)
    inverse_head = got[rows, W + 2 * K : W + 2 * K + LANE]
    inverse_tail = got[rows, W + 2 * K + 2 * LANE :]
    part[...] = (dot(inverse_head, head) + dot(inverse_tail, tail)).astype(BF16)


def ready_kernel(
    rows, panels, rhs, root, facts, low_rows, low_panels, base, spread, low_base, low_spread
):
    del facts
    for n in range(2):
        index = rows[n : n + 1, :]
        turned = panels[n].T
        picked = dot(one_hot(index, 0, W // LANE), root[...]).astype(BF16)
        base[n] = rhs[n].astype(F32) - dot(turned, picked)
        spread[n] = dot(turned, one_hot(index, W, W // LANE)).astype(BF16)
    for n in range(2):
        index = low_rows[n : n + 1, :]
        turned = low_panels[n].T
        picked = dot(one_hot(index, 0, W // LANE), root[...]).astype(BF16)
        low_base[n] = dot(turned, picked)
        low_spread[n] = dot(turned, one_hot(index, 2 * W, W // LANE)).astype(BF16)


def rows_of(mid, parent):
    return mid[pl.ds(pl.multiple_of(parent * W, W), W), :]


def sub_kernel(facts, mid, base, spread, inverse, out):
    for n in range(2):
        update = (base[n] - dot(spread[n], rows_of(mid, facts[0, 5 * n]))).astype(BF16)
        out[n] = dot(inverse[n], update).astype(BF16)


def leaf_middle_kernel(
    facts, rows, panels, rhs, root, mid, solved, from_root, base, root_own, mid_own, out, sem
):
    store = pltpu.make_async_copy(solved, out, sem)
    store.start()
    own_rows = root_own.shape[0]
    first = lax.axis_index(ROWS) * own_rows
    row = lax.broadcasted_iota(jnp.int32, (own_rows, W), 0) + first
    column = lax.broadcasted_iota(jnp.int32, (own_rows, W), 1)
    own = (row == column).astype(F32).astype(BF16)
    root_own[...] = dot(own, root[...]).astype(BF16)
    for s in range(mid_own.shape[0]):
        mid_own[s] = dot(own, mid[s * W : (s + 1) * W, :]).astype(BF16)
    for n in range(2):
        index = rows[n : n + 1, :]
        above = rows_of(mid, facts[0, 5 * n + 1])
        picked = dot(one_hot(index, W, W // LANE), above).astype(BF16)
        base[n] = rhs[n].astype(F32) - from_root[n] - dot(panels[n].T, picked)
    store.wait()


def leaf_kernel(facts, base, spread, inverse, chip, nearby, outer, out, held, done, sems):
    stores = []
    for n in range(2):
        block, member, live = (facts[0, 5 * n + i] for i in (2, 3, 4))

        @pl.when(jnp.logical_or(block == 0, block == 1))
        def _():
            held[n] = chip[2 * block + member]

        @pl.when(jnp.logical_or(block == -1, block == 2))
        def _():
            held[n] = nearby[jnp.where(block == 2, 2, 0) + member]

        @pl.when(jnp.logical_or(block == -2, block == 3))
        def _():
            held[n] = outer[member]

        update = (base[n] - dot(spread[n], held[n])).astype(BF16)
        solved = dot(inverse[n], update)
        row = lax.broadcasted_iota(jnp.int32, (W, K), 0)
        done[n] = jnp.where(row < live, solved, 0.0).astype(BF16)
        stores.append(pltpu.make_async_copy(done.at[n], out.at[n], sems.at[n]))
        stores[n].start()
    for store in stores:
        store.wait()


def per_device(
    root_inverse,
    root_rhs,
    mid_panels,
    mid_rows,
    mid_inverse,
    mid_rhs,
    parent_list,
    sub_panels,
    sub_rows,
    sub_inverse,
    sub_rhs,
    group_of,
    leaf_panels,
    leaf_rows,
    leaf_inverse,
    leaf_rhs,
    live_cols,
):
    own_rows = root_inverse.shape[0]
    total = lax.axis_size(ALL)
    parents = parent_list.reshape(-1)
    packed, facts = call(
        functools.partial(pack_kernel, total),
        (shape(own_rows, 1280), shape(1, LANE, dtype=jnp.int32)),
        [HBM] * 8,
        0,
        4 * own_rows * 1280,
        scratch=[pltpu.VMEM((own_rows, W), BF16)] * 2
        + [pltpu.SMEM(a.shape, jnp.int32) for a in (parents, group_of, live_cols)]
        + [pltpu.SemaphoreType.DMA((8,))],
        grant=60,
    )(root_inverse, root_rhs, mid_panels, mid_inverse, mid_rhs, parents, group_of, live_cols)
    got = lax.all_gather(packed, ROWS, axis=0, tiled=True)
    square, tall = shape(2, W, W), shape(2, W, K, dtype=F32)
    thin = shape(2, W, K)
    root, part = call(
        upper_kernel,
        (shape(W, K), shape(HALF, K)),
        [VMEM] * 4,
        2 * W * W * K,
        2 * W * 1280,
    )(got, mid_rows, leaf_panels, leaf_inverse)
    other = lax.ppermute(part, "y", [(i, i ^ 1) for i in range(lax.axis_size("y"))])
    base, spread, from_root, leaf_spread = call(
        ready_kernel,
        (tall, square, tall, square),
        [VMEM] * 7,
        16 * W * W * K,
        16 * W * W + 40 * W * K,
    )(sub_rows, sub_panels, sub_rhs, root, facts, leaf_rows, leaf_panels)
    mid_half = (part.astype(F32) + other.astype(F32)).astype(BF16)
    mid_half, base = lax.optimization_barrier((mid_half, base))
    mid = lax.all_gather(mid_half, ("x", "c"), axis=0, tiled=True)
    solved = call(
        sub_kernel,
        shape(2, W, K),
        [SMEM] + [VMEM] * 4,
        4 * W * W * K,
        12 * W * W + 16 * W * K,
    )(facts, mid, base, spread, sub_inverse)
    chips = total // 2
    cross = [((2 * m - 1) % total, 2 * m) for m in range(chips)]
    cross += [((2 * m + 2) % total, 2 * m + 1) for m in range(chips)]
    straight = [((2 * m - 2) % total, 2 * m) for m in range(chips)]
    straight += [((2 * m + 3) % total, 2 * m + 1) for m in range(chips)]
    inner = lax.ppermute(solved, ALL, cross)
    outer = lax.ppermute(solved, ALL, straight)
    chip = lax.all_gather(solved, "c", axis=0, tiled=True)
    leaf_base, root_own, mid_own, sub_solution = call(
        leaf_middle_kernel,
        (tall, shape(own_rows, K), shape(mid_rows.shape[0], own_rows, K), thin),
        [SMEM] + [VMEM] * 7,
        4 * W * W * K,
        8 * W * W + 24 * W * K,
        places=(VMEM,) * 3 + (HBM,),
        scratch=[pltpu.SemaphoreType.DMA],
    )(facts, leaf_rows, leaf_panels, leaf_rhs, root, mid, solved, from_root)
    inner, chip, leaf_base = lax.optimization_barrier((inner, chip, leaf_base))
    nearby = lax.all_gather(inner, "c", axis=0, tiled=True)
    leaf_solution = call(
        leaf_kernel,
        shape(2, W, K),
        [SMEM] + [VMEM] * 6,
        4 * W * W * K,
        12 * W * W + 24 * W * K,
        places=HBM,
        scratch=[pltpu.VMEM((2, W, K), BF16)] * 2 + [pltpu.SemaphoreType.DMA((2,))],
    )(facts, leaf_base, leaf_spread, leaf_inverse, chip, nearby, outer)
    return (root_own, mid_own, sub_solution, leaf_solution)


def solution(mesh):
    chips = Mesh(mesh.devices.reshape(8, 4, 8, 2), ALL)
    lower = P(ALL, None, None)
    return jax.shard_map(
        per_device,
        mesh=chips,
        in_specs=(
            P(ROWS, None),
            P(ROWS, None),
            P(None, ROWS, None),
            P(),
            P(None, ROWS, None),
            P(None, ROWS, None),
            P(),
            lower,
            P(ALL, None),
            lower,
            lower,
            P(ALL),
            lower,
            P(ALL, None),
            lower,
            lower,
            P(ALL),
        ),
        out_specs=(P(ROWS, None), P(None, ROWS, None), lower, lower),
        check_vma=False,
    )
```

```python
import functools

import jax
import jax.numpy as jnp
from jax import lax
from jax.experimental import pallas as pl
from jax.experimental.pallas import tpu as pltpu
from jax.sharding import Mesh, PartitionSpec as P

HOP = 2
ALL = ("y", "x", "z", "c")
ROWS = ("z", "c")
W = 384
K = 256
HALF = W // 2
LANE = 128
BF16 = jnp.bfloat16
F32 = jnp.float32

VMEM = pl.BlockSpec(memory_space=pltpu.VMEM)
SMEM = pl.BlockSpec(memory_space=pltpu.SMEM)
ANY = pl.BlockSpec(memory_space=pl.ANY)
HBM = pl.BlockSpec(memory_space=pltpu.HBM)


def shape(*dims, dtype=BF16):
    return jax.ShapeDtypeStruct(dims, dtype)


def call(body, outs, ins, macs, moved, places=None, scratch=(), grant=16):
    return pl.pallas_call(
        body,
        out_shape=outs,
        in_specs=ins,
        out_specs=places or jax.tree.map(lambda _: VMEM, outs),
        scratch_shapes=scratch,
        cost_estimate=pl.CostEstimate(flops=2 * macs, bytes_accessed=moved, transcendentals=0),
        compiler_params=pltpu.CompilerParams(vmem_limit_bytes=int(grant * 2**20)),
    )


def dot(a, b):
    return jnp.dot(a, b, preferred_element_type=F32)


def one_hot(index_row, first, blocks):
    spread = jnp.broadcast_to(index_row, (LANE, W)).T
    lane = lax.broadcasted_iota(jnp.int32, (W, LANE), 1) + first
    parts = [(spread == lane + LANE * j).astype(F32).astype(BF16) for j in range(blocks)]
    return jnp.concatenate(parts, axis=1)


def pack_kernel(
    total,
    root_inverse,
    root_rhs,
    panels,
    inverses,
    rhs,
    parents_all,
    groups_all,
    live_all,
    out,
    facts,
    panel,
    inverse,
    parents,
    groups,
    live,
    sems,
):
    node = lax.axis_index("x")
    side = lax.rem(lax.axis_index("y"), 2)
    here = lax.axis_index(ALL)
    pairs = [
        (groups_all, groups),
        (parents_all, parents),
        (live_all, live),
        (panels.at[node], panel),
        (inverses.at[node], inverse),
        (root_inverse, out.at[:, :W]),
        (root_rhs, out.at[:, W : W + K]),
        (rhs.at[node], out.at[:, W + K : W + 2 * K]),
    ]
    copies = [pltpu.make_async_copy(a, b, sems.at[i]) for i, (a, b) in enumerate(pairs)]
    for copy in copies:
        copy.start()
    for copy in copies:
        copy.wait()
    values = []
    for n in range(2):
        group = groups[n]
        block = lax.rem(group // 2 - here + total + HOP, total) - HOP + lax.rem(here, 2)
        values += [parents[2 * here + n], parents[group], block, lax.rem(group, 2), live[n]]
    place = lax.broadcasted_iota(jnp.int32, facts.shape, 1)
    row = jnp.zeros(facts.shape, jnp.int32)
    for i, value in enumerate(values):
        row = jnp.where(place == i, value, row)
    facts[...] = row

    def half(array):
        return jnp.where(side == 0, array[:, :HALF], array[:, HALF:])

    inverse_half = half(inverse[...])
    out[:, W + 2 * K :] = jnp.concatenate(
        [inverse_half[:, :LANE], half(panel[...]), inverse_half[:, LANE:]], axis=1
    )


def upper_kernel(got, mid_rows, panels, inverses, root, part):
    del panels, inverses
    side = lax.rem(lax.axis_index("y"), 2)
    core = lax.axis_index("c")
    mid_index = mid_rows[pl.ds(lax.axis_index("x"), 1), :]
    solved = dot(got[:, :W], got[:, W : W + K]).astype(BF16)
    root[...] = solved
    picked = dot(one_hot(mid_index, 0, W // LANE), solved).astype(BF16)
    products = dot(got[:, W + 2 * K + LANE :].T, picked)
    first = pl.multiple_of(side * HALF, 64)
    rhs = got[pl.ds(first, HALF), W + K : W + 2 * K].astype(F32)
    update = (rhs - products[:HALF]).astype(BF16)
    head = update[:LANE]
    tail = jnp.concatenate([jnp.zeros((LANE // 2, K), BF16), update[LANE:]], axis=0)
    rows = pl.ds(pl.multiple_of(core * HALF, 64), HALF)
    inverse_head = got[rows, W + 2 * K : W + 2 * K + LANE]
    inverse_tail = got[rows, W + 2 * K + 2 * LANE :]
    part[...] = (dot(inverse_head, head) + dot(inverse_tail, tail)).astype(BF16)


def ready_kernel(
    rows, panels, rhs, root, facts, low_rows, low_panels, base, spread, low_base, low_spread
):
    del facts
    for n in range(2):
        index = rows[n : n + 1, :]
        turned = panels[n].T
        picked = dot(one_hot(index, 0, W // LANE), root[...]).astype(BF16)
        base[n] = rhs[n].astype(F32) - dot(turned, picked)
        spread[n] = dot(turned, one_hot(index, W, W // LANE)).astype(BF16)
    for n in range(2):
        index = low_rows[n : n + 1, :]
        turned = low_panels[n].T
        picked = dot(one_hot(index, 0, W // LANE), root[...]).astype(BF16)
        low_base[n] = dot(turned, picked)
        low_spread[n] = dot(turned, one_hot(index, 2 * W, W // LANE)).astype(BF16)


def rows_of(mid, parent):
    return mid[pl.ds(pl.multiple_of(parent * W, W), W), :]


def sub_kernel(facts, mid, base, spread, inverse, out):
    updates = [
        (base[n] - dot(spread[n], rows_of(mid, facts[0, 5 * n]))).astype(BF16) for n in range(2)
    ]
    for n in range(2):
        out[n] = dot(inverse[n], updates[n]).astype(BF16)


def leaf_middle_kernel(
    facts, rows, panels, rhs, root, mid, solved, from_root, base, root_own, mid_own, out, sem
):
    store = pltpu.make_async_copy(solved, out, sem)
    store.start()
    own_rows = root_own.shape[0]
    first = lax.axis_index(ROWS) * own_rows
    row = lax.broadcasted_iota(jnp.int32, (own_rows, W), 0) + first
    column = lax.broadcasted_iota(jnp.int32, (own_rows, W), 1)
    own = (row == column).astype(F32).astype(BF16)
    root_own[...] = dot(own, root[...]).astype(BF16)
    for s in range(mid_own.shape[0]):
        mid_own[s] = dot(own, mid[s * W : (s + 1) * W, :]).astype(BF16)
    for n in range(2):
        index = rows[n : n + 1, :]
        above = rows_of(mid, facts[0, 5 * n + 1])
        picked = dot(one_hot(index, W, W // LANE), above).astype(BF16)
        base[n] = rhs[n].astype(F32) - from_root[n] - dot(panels[n].T, picked)
    store.wait()


def leaf_kernel(facts, base, spread, inverse, chip, nearby, outer, out, held, done, sems):
    for n in range(2):
        block, member = facts[0, 5 * n + 2], facts[0, 5 * n + 3]

        @pl.when(jnp.logical_or(block == 0, block == 1))
        def _():
            held[n] = chip[2 * block + member]

        @pl.when(jnp.logical_or(block == -1, block == 2))
        def _():
            held[n] = nearby[jnp.where(block == 2, 2, 0) + member]

        @pl.when(jnp.logical_or(block == -2, block == 3))
        def _():
            held[n] = outer[member]

    row = lax.broadcasted_iota(jnp.int32, (W, K), 0)
    updates = [(base[n] - dot(spread[n], held[n])).astype(BF16) for n in range(2)]
    stores = []
    for n in range(2):
        solved = dot(inverse[n], updates[n])
        done[n] = jnp.where(row < facts[0, 5 * n + 4], solved, 0.0).astype(BF16)
        stores.append(pltpu.make_async_copy(done.at[n], out.at[n], sems.at[n]))
        stores[n].start()
    for store in stores:
        store.wait()


def per_device(
    root_inverse,
    root_rhs,
    mid_panels,
    mid_rows,
    mid_inverse,
    mid_rhs,
    parent_list,
    sub_panels,
    sub_rows,
    sub_inverse,
    sub_rhs,
    group_of,
    leaf_panels,
    leaf_rows,
    leaf_inverse,
    leaf_rhs,
    live_cols,
):
    own_rows = root_inverse.shape[0]
    total = lax.axis_size(ALL)
    parents = parent_list.reshape(-1)
    packed, facts = call(
        functools.partial(pack_kernel, total),
        (shape(own_rows, 1280), shape(1, LANE, dtype=jnp.int32)),
        [HBM] * 8,
        0,
        4 * own_rows * 1280,
        scratch=[pltpu.VMEM((own_rows, W), BF16)] * 2
        + [pltpu.SMEM(a.shape, jnp.int32) for a in (parents, group_of, live_cols)]
        + [pltpu.SemaphoreType.DMA((8,))],
        grant=60,
    )(root_inverse, root_rhs, mid_panels, mid_inverse, mid_rhs, parents, group_of, live_cols)
    got = lax.all_gather(packed, ROWS, axis=0, tiled=True)
    square, tall = shape(2, W, W), shape(2, W, K, dtype=F32)
    thin = shape(2, W, K)
    root, part = call(
        upper_kernel,
        (shape(W, K), shape(HALF, K)),
        [VMEM] * 4,
        2 * W * W * K,
        2 * W * 1280,
    )(got, mid_rows, leaf_panels, leaf_inverse)
    other = lax.ppermute(part, "y", [(i, i ^ 1) for i in range(lax.axis_size("y"))])
    base, spread, from_root, leaf_spread = call(
        ready_kernel,
        (tall, square, tall, square),
        [VMEM] * 7,
        16 * W * W * K,
        16 * W * W + 40 * W * K,
    )(sub_rows, sub_panels, sub_rhs, root, facts, leaf_rows, leaf_panels)
    mid_half = (part.astype(F32) + other.astype(F32)).astype(BF16)
    mid_half, base = lax.optimization_barrier((mid_half, base))
    mid = lax.all_gather(mid_half, ("x", "c"), axis=0, tiled=True)
    solved = call(
        sub_kernel,
        shape(2, W, K),
        [SMEM] + [VMEM] * 4,
        4 * W * W * K,
        12 * W * W + 16 * W * K,
    )(facts, mid, base, spread, sub_inverse)
    chips = total // 2
    cross = [((2 * m - 1) % total, 2 * m) for m in range(chips)]
    cross += [((2 * m + 2) % total, 2 * m + 1) for m in range(chips)]
    straight = [((2 * m - 2) % total, 2 * m) for m in range(chips)]
    straight += [((2 * m + 3) % total, 2 * m + 1) for m in range(chips)]
    inner = lax.ppermute(solved, ALL, cross)
    outer = lax.ppermute(solved, ALL, straight)
    chip = lax.all_gather(solved, "c", axis=0, tiled=True)
    leaf_base, root_own, mid_own, sub_solution = call(
        leaf_middle_kernel,
        (tall, shape(own_rows, K), shape(mid_rows.shape[0], own_rows, K), thin),
        [SMEM] + [VMEM] * 7,
        4 * W * W * K,
        8 * W * W + 24 * W * K,
        places=(VMEM,) * 3 + (HBM,),
        scratch=[pltpu.SemaphoreType.DMA],
    )(facts, leaf_rows, leaf_panels, leaf_rhs, root, mid, solved, from_root)
    inner, chip, leaf_base = lax.optimization_barrier((inner, chip, leaf_base))
    nearby = lax.all_gather(inner, "c", axis=0, tiled=True)
    leaf_solution = call(
        leaf_kernel,
        shape(2, W, K),
        [SMEM] + [VMEM] * 6,
        4 * W * W * K,
        12 * W * W + 24 * W * K,
        places=HBM,
        scratch=[pltpu.VMEM((2, W, K), BF16)] * 2 + [pltpu.SemaphoreType.DMA((2,))],
    )(facts, leaf_base, leaf_spread, leaf_inverse, chip, nearby, outer)
    return (root_own, mid_own, sub_solution, leaf_solution)


def solution(mesh):
    chips = Mesh(mesh.devices.reshape(8, 4, 8, 2), ALL)
    lower = P(ALL, None, None)
    return jax.shard_map(
        per_device,
        mesh=chips,
        in_specs=(
            P(ROWS, None),
            P(ROWS, None),
            P(None, ROWS, None),
            P(),
            P(None, ROWS, None),
            P(None, ROWS, None),
            P(),
            lower,
            P(ALL, None),
            lower,
            lower,
            P(ALL),
            lower,
            P(ALL, None),
            lower,
            lower,
            P(ALL),
        ),
        out_specs=(P(ROWS, None), P(None, ROWS, None), lower, lower),
        check_vma=False,
    )
```

```python
import functools

import jax
import jax.numpy as jnp
from jax import lax
from jax.experimental import pallas as pl
from jax.experimental.pallas import tpu as pltpu
from jax.sharding import Mesh, PartitionSpec as P

HOP = 2
ALL = ("y", "x", "z", "c")
ROWS = ("z", "c")
W = 384
K = 256
HALF = W // 2
LANE = 128
BF16 = jnp.bfloat16
F32 = jnp.float32

VMEM = pl.BlockSpec(memory_space=pltpu.VMEM)
SMEM = pl.BlockSpec(memory_space=pltpu.SMEM)
ANY = pl.BlockSpec(memory_space=pl.ANY)
HBM = pl.BlockSpec(memory_space=pltpu.HBM)


def shape(*dims, dtype=BF16):
    return jax.ShapeDtypeStruct(dims, dtype)


def call(body, outs, ins, macs, moved, places=None, scratch=(), grant=16):
    return pl.pallas_call(
        body,
        out_shape=outs,
        in_specs=ins,
        out_specs=places or jax.tree.map(lambda _: VMEM, outs),
        scratch_shapes=scratch,
        cost_estimate=pl.CostEstimate(flops=2 * macs, bytes_accessed=moved, transcendentals=0),
        compiler_params=pltpu.CompilerParams(vmem_limit_bytes=int(grant * 2**20)),
    )


def dot(a, b):
    return jnp.dot(a, b, preferred_element_type=F32)


def one_hot(index_row, first, blocks):
    spread = jnp.broadcast_to(index_row, (LANE, W)).T
    lane = lax.broadcasted_iota(jnp.int32, (W, LANE), 1) + first
    parts = [(spread == lane + LANE * j).astype(F32).astype(BF16) for j in range(blocks)]
    return jnp.concatenate(parts, axis=1)


def pack_kernel(
    total,
    root_inverse,
    root_rhs,
    panels,
    inverses,
    rhs,
    parents_all,
    groups_all,
    live_all,
    out,
    facts,
    panel,
    inverse,
    parents,
    groups,
    live,
    sems,
):
    node = lax.axis_index("x")
    side = lax.rem(lax.axis_index("y"), 2)
    here = lax.axis_index(ALL)
    pairs = [
        (groups_all, groups),
        (parents_all, parents),
        (live_all, live),
        (panels.at[node], panel),
        (inverses.at[node], inverse),
        (root_inverse, out.at[:, :W]),
        (root_rhs, out.at[:, W : W + K]),
        (rhs.at[node], out.at[:, W + K : W + 2 * K]),
    ]
    copies = [pltpu.make_async_copy(a, b, sems.at[i]) for i, (a, b) in enumerate(pairs)]
    for copy in copies:
        copy.start()
    for copy in copies:
        copy.wait()
    values = []
    for n in range(2):
        group = groups[n]
        block = lax.rem(group // 2 - here + total + HOP, total) - HOP + lax.rem(here, 2)
        values += [parents[2 * here + n], parents[group], block, lax.rem(group, 2), live[n]]
    place = lax.broadcasted_iota(jnp.int32, facts.shape, 1)
    row = jnp.zeros(facts.shape, jnp.int32)
    for i, value in enumerate(values):
        row = jnp.where(place == i, value, row)
    facts[...] = row

    def half(array):
        return jnp.where(side == 0, array[:, :HALF], array[:, HALF:])

    inverse_half = half(inverse[...])
    out[:, W + 2 * K :] = jnp.concatenate(
        [inverse_half[:, :LANE], half(panel[...]), inverse_half[:, LANE:]], axis=1
    )


def upper_kernel(got, mid_rows, panels, inverses, root, part):
    del panels, inverses
    side = lax.rem(lax.axis_index("y"), 2)
    core = lax.axis_index("c")
    mid_index = mid_rows[pl.ds(lax.axis_index("x"), 1), :]
    solved = dot(got[:, :W], got[:, W : W + K]).astype(BF16)
    root[...] = solved
    picked = dot(one_hot(mid_index, 0, W // LANE), solved).astype(BF16)
    products = dot(got[:, W + 2 * K + LANE :].T, picked)
    first = pl.multiple_of(side * HALF, 64)
    rhs = got[pl.ds(first, HALF), W + K : W + 2 * K].astype(F32)
    update = (rhs - products[:HALF]).astype(BF16)
    head = update[:LANE]
    tail = jnp.concatenate([jnp.zeros((LANE // 2, K), BF16), update[LANE:]], axis=0)
    rows = pl.ds(pl.multiple_of(core * HALF, 64), HALF)
    inverse_head = got[rows, W + 2 * K : W + 2 * K + LANE]
    inverse_tail = got[rows, W + 2 * K + 2 * LANE :]
    part[...] = (dot(inverse_head, head) + dot(inverse_tail, tail)).astype(BF16)


def ready_kernel(
    rows, panels, rhs, root, facts, low_rows, low_panels, base, spread, low_base, low_spread
):
    del facts
    for n in range(2):
        index = rows[n : n + 1, :]
        turned = panels[n].T
        picked = dot(one_hot(index, 0, W // LANE), root[...]).astype(BF16)
        base[n] = rhs[n].astype(F32) - dot(turned, picked)
        spread[n] = dot(turned, one_hot(index, W, W // LANE)).astype(BF16)
    for n in range(2):
        index = low_rows[n : n + 1, :]
        turned = low_panels[n].T
        picked = dot(one_hot(index, 0, W // LANE), root[...]).astype(BF16)
        low_base[n] = dot(turned, picked)
        low_spread[n] = dot(turned, one_hot(index, 2 * W, W // LANE)).astype(BF16)


def fact(facts, place):
    lane = lax.broadcasted_iota(jnp.int32, facts.shape, 1)
    return jnp.sum(jnp.where(lane == place, facts[...], 0))


def rows_of(mid, parent):
    return mid[pl.ds(pl.multiple_of(parent * W, W), W), :]


def sub_kernel(facts, mid, base, spread, inverse, out):
    updates = [
        (base[n] - dot(spread[n], rows_of(mid, fact(facts, 5 * n)))).astype(BF16) for n in range(2)
    ]
    for n in range(2):
        out[n] = dot(inverse[n], updates[n]).astype(BF16)


def leaf_middle_kernel(
    facts, rows, panels, rhs, root, mid, solved, from_root, base, root_own, mid_own, out, sem
):
    store = pltpu.make_async_copy(solved, out, sem)
    store.start()
    own_rows = root_own.shape[0]
    first = lax.axis_index(ROWS) * own_rows
    row = lax.broadcasted_iota(jnp.int32, (own_rows, W), 0) + first
    column = lax.broadcasted_iota(jnp.int32, (own_rows, W), 1)
    own = (row == column).astype(F32).astype(BF16)
    root_own[...] = dot(own, root[...]).astype(BF16)
    for s in range(mid_own.shape[0]):
        mid_own[s] = dot(own, mid[s * W : (s + 1) * W, :]).astype(BF16)
    for n in range(2):
        index = rows[n : n + 1, :]
        above = rows_of(mid, fact(facts, 5 * n + 1))
        picked = dot(one_hot(index, W, W // LANE), above).astype(BF16)
        base[n] = rhs[n].astype(F32) - from_root[n] - dot(panels[n].T, picked)
    store.wait()


def leaf_kernel(facts, base, spread, inverse, chip, nearby, outer, out, held, done, sems):
    for n in range(2):
        block, member = fact(facts, 5 * n + 2), fact(facts, 5 * n + 3)

        @pl.when(jnp.logical_or(block == 0, block == 1))
        def _():
            held[n] = chip[2 * block + member]

        @pl.when(jnp.logical_or(block == -1, block == 2))
        def _():
            held[n] = nearby[jnp.where(block == 2, 2, 0) + member]

        @pl.when(jnp.logical_or(block == -2, block == 3))
        def _():
            held[n] = outer[member]

    row = lax.broadcasted_iota(jnp.int32, (W, K), 0)
    updates = [(base[n] - dot(spread[n], held[n])).astype(BF16) for n in range(2)]
    stores = []
    for n in range(2):
        solved = dot(inverse[n], updates[n])
        done[n] = jnp.where(row < fact(facts, 5 * n + 4), solved, 0.0).astype(BF16)
        stores.append(pltpu.make_async_copy(done.at[n], out.at[n], sems.at[n]))
        stores[n].start()
    for store in stores:
        store.wait()


def per_device(
    root_inverse,
    root_rhs,
    mid_panels,
    mid_rows,
    mid_inverse,
    mid_rhs,
    parent_list,
    sub_panels,
    sub_rows,
    sub_inverse,
    sub_rhs,
    group_of,
    leaf_panels,
    leaf_rows,
    leaf_inverse,
    leaf_rhs,
    live_cols,
):
    own_rows = root_inverse.shape[0]
    total = lax.axis_size(ALL)
    parents = parent_list.reshape(-1)
    packed, facts = call(
        functools.partial(pack_kernel, total),
        (shape(own_rows, 1280), shape(1, LANE, dtype=jnp.int32)),
        [HBM] * 8,
        0,
        4 * own_rows * 1280,
        scratch=[pltpu.VMEM((own_rows, W), BF16)] * 2
        + [pltpu.SMEM(a.shape, jnp.int32) for a in (parents, group_of, live_cols)]
        + [pltpu.SemaphoreType.DMA((8,))],
        grant=60,
    )(root_inverse, root_rhs, mid_panels, mid_inverse, mid_rhs, parents, group_of, live_cols)
    got = lax.all_gather(packed, ROWS, axis=0, tiled=True)
    square, tall = shape(2, W, W), shape(2, W, K, dtype=F32)
    thin = shape(2, W, K)
    root, part = call(
        upper_kernel,
        (shape(W, K), shape(HALF, K)),
        [VMEM] * 4,
        2 * W * W * K,
        2 * W * 1280,
    )(got, mid_rows, leaf_panels, leaf_inverse)
    other = lax.ppermute(part, "y", [(i, i ^ 1) for i in range(lax.axis_size("y"))])
    base, spread, from_root, leaf_spread = call(
        ready_kernel,
        (tall, square, tall, square),
        [VMEM] * 7,
        16 * W * W * K,
        16 * W * W + 40 * W * K,
    )(sub_rows, sub_panels, sub_rhs, root, facts, leaf_rows, leaf_panels)
    mid_half = (part.astype(F32) + other.astype(F32)).astype(BF16)
    mid_half, base = lax.optimization_barrier((mid_half, base))
    mid = lax.all_gather(mid_half, ("x", "c"), axis=0, tiled=True)
    solved = call(
        sub_kernel,
        shape(2, W, K),
        [VMEM] * 5,
        4 * W * W * K,
        12 * W * W + 16 * W * K,
    )(facts, mid, base, spread, sub_inverse)
    chips = total // 2
    cross = [((2 * m - 1) % total, 2 * m) for m in range(chips)]
    cross += [((2 * m + 2) % total, 2 * m + 1) for m in range(chips)]
    straight = [((2 * m - 2) % total, 2 * m) for m in range(chips)]
    straight += [((2 * m + 3) % total, 2 * m + 1) for m in range(chips)]
    inner = lax.ppermute(solved, ALL, cross)
    outer = lax.ppermute(solved, ALL, straight)
    chip = lax.all_gather(solved, "c", axis=0, tiled=True)
    leaf_base, root_own, mid_own, sub_solution = call(
        leaf_middle_kernel,
        (tall, shape(own_rows, K), shape(mid_rows.shape[0], own_rows, K), thin),
        [VMEM] * 8,
        4 * W * W * K,
        8 * W * W + 24 * W * K,
        places=(VMEM,) * 3 + (HBM,),
        scratch=[pltpu.SemaphoreType.DMA],
    )(facts, leaf_rows, leaf_panels, leaf_rhs, root, mid, solved, from_root)
    inner, chip, leaf_base = lax.optimization_barrier((inner, chip, leaf_base))
    nearby = lax.all_gather(inner, "c", axis=0, tiled=True)
    leaf_solution = call(
        leaf_kernel,
        shape(2, W, K),
        [VMEM] * 7,
        4 * W * W * K,
        12 * W * W + 24 * W * K,
        places=HBM,
        scratch=[pltpu.VMEM((2, W, K), BF16)] * 2 + [pltpu.SemaphoreType.DMA((2,))],
    )(facts, leaf_base, leaf_spread, leaf_inverse, chip, nearby, outer)
    return (root_own, mid_own, sub_solution, leaf_solution)


def solution(mesh):
    chips = Mesh(mesh.devices.reshape(8, 4, 8, 2), ALL)
    lower = P(ALL, None, None)
    return jax.shard_map(
        per_device,
        mesh=chips,
        in_specs=(
            P(ROWS, None),
            P(ROWS, None),
            P(None, ROWS, None),
            P(),
            P(None, ROWS, None),
            P(None, ROWS, None),
            P(),
            lower,
            P(ALL, None),
            lower,
            lower,
            P(ALL),
            lower,
            P(ALL, None),
            lower,
            lower,
            P(ALL),
        ),
        out_specs=(P(ROWS, None), P(None, ROWS, None), lower, lower),
        check_vma=False,
    )
```

```python
import functools

import jax
import jax.numpy as jnp
from jax import lax
from jax.experimental import pallas as pl
from jax.experimental.pallas import tpu as pltpu
from jax.sharding import Mesh, PartitionSpec as P

HOP = 2
ALL = ("y", "x", "z", "c")
ROWS = ("z", "c")
W = 384
K = 256
HALF = W // 2
LANE = 128
BF16 = jnp.bfloat16
F32 = jnp.float32

VMEM = pl.BlockSpec(memory_space=pltpu.VMEM)
SMEM = pl.BlockSpec(memory_space=pltpu.SMEM)
ANY = pl.BlockSpec(memory_space=pl.ANY)
HBM = pl.BlockSpec(memory_space=pltpu.HBM)


def shape(*dims, dtype=BF16):
    return jax.ShapeDtypeStruct(dims, dtype)


def call(body, outs, ins, macs, moved, places=None, scratch=(), grant=16):
    return pl.pallas_call(
        body,
        out_shape=outs,
        in_specs=ins,
        out_specs=places or jax.tree.map(lambda _: VMEM, outs),
        scratch_shapes=scratch,
        cost_estimate=pl.CostEstimate(flops=2 * macs, bytes_accessed=moved, transcendentals=0),
        compiler_params=pltpu.CompilerParams(vmem_limit_bytes=int(grant * 2**20)),
    )


def dot(a, b):
    return jnp.dot(a, b, preferred_element_type=F32)


def one_hot(index_row, first, blocks):
    spread = jnp.broadcast_to(index_row, (LANE, W)).T
    lane = lax.broadcasted_iota(jnp.int32, (W, LANE), 1) + first
    parts = [(spread == lane + LANE * j).astype(F32).astype(BF16) for j in range(blocks)]
    return jnp.concatenate(parts, axis=1)


def pack_kernel(
    total,
    root_inverse,
    root_rhs,
    panels,
    inverses,
    rhs,
    parents_all,
    groups_all,
    live_all,
    out,
    facts,
    panel,
    inverse,
    parents,
    groups,
    live,
    sems,
):
    node = lax.axis_index("x")
    side = lax.rem(lax.axis_index("y"), 2)
    here = lax.axis_index(ALL)
    pairs = [
        (groups_all, groups),
        (parents_all, parents),
        (live_all, live),
        (panels.at[node], panel),
        (inverses.at[node], inverse),
        (root_inverse, out.at[:, :W]),
        (root_rhs, out.at[:, W : W + K]),
        (rhs.at[node], out.at[:, W + K : W + 2 * K]),
    ]
    copies = [pltpu.make_async_copy(a, b, sems.at[i]) for i, (a, b) in enumerate(pairs)]
    for copy in copies:
        copy.start()
    for copy in copies:
        copy.wait()
    values = []
    for n in range(2):
        group = groups[n]
        block = lax.rem(group // 2 - here + total + HOP, total) - HOP + lax.rem(here, 2)
        values += [parents[2 * here + n], parents[group], block, lax.rem(group, 2), live[n]]
    place = lax.broadcasted_iota(jnp.int32, facts.shape, 1)
    row = jnp.zeros(facts.shape, jnp.int32)
    for i, value in enumerate(values):
        row = jnp.where(place == i, value, row)
    facts[...] = row

    def half(array):
        return jnp.where(side == 0, array[:, :HALF], array[:, HALF:])

    inverse_half = half(inverse[...])
    out[:, W + 2 * K :] = jnp.concatenate(
        [inverse_half[:, :LANE], half(panel[...]), inverse_half[:, LANE:]], axis=1
    )


def upper_kernel(got, mid_rows, panels, inverses, root, part):
    del panels, inverses
    side = lax.rem(lax.axis_index("y"), 2)
    core = lax.axis_index("c")
    mid_index = mid_rows[pl.ds(lax.axis_index("x"), 1), :]
    solved = dot(got[:, :W], got[:, W : W + K]).astype(BF16)
    root[...] = solved
    spread = dot(got[:, W + 2 * K + LANE :].T, one_hot(mid_index, 0, W // LANE)).astype(BF16)
    products = dot(spread, solved)
    first = pl.multiple_of(side * HALF, 64)
    rhs = got[pl.ds(first, HALF), W + K : W + 2 * K].astype(F32)
    update = (rhs - products[:HALF]).astype(BF16)
    head = update[:LANE]
    tail = jnp.concatenate([jnp.zeros((LANE // 2, K), BF16), update[LANE:]], axis=0)
    rows = pl.ds(pl.multiple_of(core * HALF, 64), HALF)
    inverse_head = got[rows, W + 2 * K : W + 2 * K + LANE]
    inverse_tail = got[rows, W + 2 * K + 2 * LANE :]
    part[...] = (dot(inverse_head, head) + dot(inverse_tail, tail)).astype(BF16)


def ready_kernel(
    rows, panels, rhs, root, facts, low_rows, low_panels, base, spread, low_base, low_spread
):
    del facts
    for n in range(2):
        index = rows[n : n + 1, :]
        turned = panels[n].T
        picked = dot(one_hot(index, 0, W // LANE), root[...]).astype(BF16)
        base[n] = rhs[n].astype(F32) - dot(turned, picked)
        spread[n] = dot(turned, one_hot(index, W, W // LANE)).astype(BF16)
    for n in range(2):
        index = low_rows[n : n + 1, :]
        turned = low_panels[n].T
        picked = dot(one_hot(index, 0, W // LANE), root[...]).astype(BF16)
        low_base[n] = dot(turned, picked)
        low_spread[n] = dot(turned, one_hot(index, 2 * W, W // LANE)).astype(BF16)


def fact(facts, place):
    lane = lax.broadcasted_iota(jnp.int32, facts.shape, 1)
    return jnp.sum(jnp.where(lane == place, facts[...], 0))


def rows_of(mid, parent):
    return mid[pl.ds(pl.multiple_of(parent * W, W), W), :]


def sub_kernel(facts, mid, base, spread, inverse, out):
    updates = [
        (base[n] - dot(spread[n], rows_of(mid, fact(facts, 5 * n)))).astype(BF16) for n in range(2)
    ]
    for n in range(2):
        out[n] = dot(inverse[n], updates[n]).astype(BF16)


def leaf_middle_kernel(
    facts, rows, panels, rhs, root, mid, solved, from_root, base, root_own, mid_own, out, sem
):
    store = pltpu.make_async_copy(solved, out, sem)
    store.start()
    own_rows = root_own.shape[0]
    first = lax.axis_index(ROWS) * own_rows
    row = lax.broadcasted_iota(jnp.int32, (own_rows, W), 0) + first
    column = lax.broadcasted_iota(jnp.int32, (own_rows, W), 1)
    own = (row == column).astype(F32).astype(BF16)
    root_own[...] = dot(own, root[...]).astype(BF16)
    for s in range(mid_own.shape[0]):
        mid_own[s] = dot(own, mid[s * W : (s + 1) * W, :]).astype(BF16)
    for n in range(2):
        index = rows[n : n + 1, :]
        above = rows_of(mid, fact(facts, 5 * n + 1))
        picked = dot(one_hot(index, W, W // LANE), above).astype(BF16)
        base[n] = rhs[n].astype(F32) - from_root[n] - dot(panels[n].T, picked)
    store.wait()


def leaf_kernel(facts, base, spread, inverse, chip, nearby, outer, out, held, done, sems):
    for n in range(2):
        block, member = fact(facts, 5 * n + 2), fact(facts, 5 * n + 3)

        @pl.when(jnp.logical_or(block == 0, block == 1))
        def _():
            held[n] = chip[2 * block + member]

        @pl.when(jnp.logical_or(block == -1, block == 2))
        def _():
            held[n] = nearby[jnp.where(block == 2, 2, 0) + member]

        @pl.when(jnp.logical_or(block == -2, block == 3))
        def _():
            held[n] = outer[member]

    row = lax.broadcasted_iota(jnp.int32, (W, K), 0)
    updates = [(base[n] - dot(spread[n], held[n])).astype(BF16) for n in range(2)]
    stores = []
    for n in range(2):
        solved = dot(inverse[n], updates[n])
        done[n] = jnp.where(row < fact(facts, 5 * n + 4), solved, 0.0).astype(BF16)
        stores.append(pltpu.make_async_copy(done.at[n], out.at[n], sems.at[n]))
        stores[n].start()
    for store in stores:
        store.wait()


def per_device(
    root_inverse,
    root_rhs,
    mid_panels,
    mid_rows,
    mid_inverse,
    mid_rhs,
    parent_list,
    sub_panels,
    sub_rows,
    sub_inverse,
    sub_rhs,
    group_of,
    leaf_panels,
    leaf_rows,
    leaf_inverse,
    leaf_rhs,
    live_cols,
):
    own_rows = root_inverse.shape[0]
    total = lax.axis_size(ALL)
    parents = parent_list.reshape(-1)
    packed, facts = call(
        functools.partial(pack_kernel, total),
        (shape(own_rows, 1280), shape(1, LANE, dtype=jnp.int32)),
        [HBM] * 8,
        0,
        4 * own_rows * 1280,
        scratch=[pltpu.VMEM((own_rows, W), BF16)] * 2
        + [pltpu.SMEM(a.shape, jnp.int32) for a in (parents, group_of, live_cols)]
        + [pltpu.SemaphoreType.DMA((8,))],
        grant=60,
    )(root_inverse, root_rhs, mid_panels, mid_inverse, mid_rhs, parents, group_of, live_cols)
    got = lax.all_gather(packed, ROWS, axis=0, tiled=True)
    square, tall = shape(2, W, W), shape(2, W, K, dtype=F32)
    thin = shape(2, W, K)
    root, part = call(
        upper_kernel,
        (shape(W, K), shape(HALF, K)),
        [VMEM] * 4,
        2 * W * W * K,
        2 * W * 1280,
    )(got, mid_rows, leaf_panels, leaf_inverse)
    other = lax.ppermute(part, "y", [(i, i ^ 1) for i in range(lax.axis_size("y"))])
    base, spread, from_root, leaf_spread = call(
        ready_kernel,
        (tall, square, tall, square),
        [VMEM] * 7,
        16 * W * W * K,
        16 * W * W + 40 * W * K,
    )(sub_rows, sub_panels, sub_rhs, root, facts, leaf_rows, leaf_panels)
    mid_half = (part.astype(F32) + other.astype(F32)).astype(BF16)
    mid_half, base = lax.optimization_barrier((mid_half, base))
    mid = lax.all_gather(mid_half, ("x", "c"), axis=0, tiled=True)
    solved = call(
        sub_kernel,
        shape(2, W, K),
        [VMEM] * 5,
        4 * W * W * K,
        12 * W * W + 16 * W * K,
    )(facts, mid, base, spread, sub_inverse)
    chips = total // 2
    cross = [((2 * m - 1) % total, 2 * m) for m in range(chips)]
    cross += [((2 * m + 2) % total, 2 * m + 1) for m in range(chips)]
    straight = [((2 * m - 2) % total, 2 * m) for m in range(chips)]
    straight += [((2 * m + 3) % total, 2 * m + 1) for m in range(chips)]
    inner = lax.ppermute(solved, ALL, cross)
    outer = lax.ppermute(solved, ALL, straight)
    chip = lax.all_gather(solved, "c", axis=0, tiled=True)
    leaf_base, root_own, mid_own, sub_solution = call(
        leaf_middle_kernel,
        (tall, shape(own_rows, K), shape(mid_rows.shape[0], own_rows, K), thin),
        [VMEM] * 8,
        4 * W * W * K,
        8 * W * W + 24 * W * K,
        places=(VMEM,) * 3 + (HBM,),
        scratch=[pltpu.SemaphoreType.DMA],
    )(facts, leaf_rows, leaf_panels, leaf_rhs, root, mid, solved, from_root)
    inner, chip, leaf_base = lax.optimization_barrier((inner, chip, leaf_base))
    nearby = lax.all_gather(inner, "c", axis=0, tiled=True)
    leaf_solution = call(
        leaf_kernel,
        shape(2, W, K),
        [VMEM] * 7,
        4 * W * W * K,
        12 * W * W + 24 * W * K,
        places=HBM,
        scratch=[pltpu.VMEM((2, W, K), BF16)] * 2 + [pltpu.SemaphoreType.DMA((2,))],
    )(facts, leaf_base, leaf_spread, leaf_inverse, chip, nearby, outer)
    return (root_own, mid_own, sub_solution, leaf_solution)


def solution(mesh):
    chips = Mesh(mesh.devices.reshape(8, 4, 8, 2), ALL)
    lower = P(ALL, None, None)
    return jax.shard_map(
        per_device,
        mesh=chips,
        in_specs=(
            P(ROWS, None),
            P(ROWS, None),
            P(None, ROWS, None),
            P(),
            P(None, ROWS, None),
            P(None, ROWS, None),
            P(),
            lower,
            P(ALL, None),
            lower,
            lower,
            P(ALL),
            lower,
            P(ALL, None),
            lower,
            lower,
            P(ALL),
        ),
        out_specs=(P(ROWS, None), P(None, ROWS, None), lower, lower),
        check_vma=False,
    )
```

```python
import functools

import jax
import jax.numpy as jnp
from jax import lax
from jax.experimental import pallas as pl
from jax.experimental.pallas import tpu as pltpu
from jax.sharding import Mesh, PartitionSpec as P

HOP = 2
ALL = ("y", "x", "z", "c")
ROWS = ("z", "c")
W = 384
K = 256
HALF = W // 2
LANE = 128
BF16 = jnp.bfloat16
F32 = jnp.float32

VMEM = pl.BlockSpec(memory_space=pltpu.VMEM)
SMEM = pl.BlockSpec(memory_space=pltpu.SMEM)
ANY = pl.BlockSpec(memory_space=pl.ANY)
HBM = pl.BlockSpec(memory_space=pltpu.HBM)


def shape(*dims, dtype=BF16):
    return jax.ShapeDtypeStruct(dims, dtype)


def call(body, outs, ins, macs, moved, places=None, scratch=(), grant=16):
    return pl.pallas_call(
        body,
        out_shape=outs,
        in_specs=ins,
        out_specs=places or jax.tree.map(lambda _: VMEM, outs),
        scratch_shapes=scratch,
        cost_estimate=pl.CostEstimate(flops=2 * macs, bytes_accessed=moved, transcendentals=0),
        compiler_params=pltpu.CompilerParams(vmem_limit_bytes=int(grant * 2**20)),
    )


def dot(a, b):
    return jnp.dot(a, b, preferred_element_type=F32)


def one_hot(index_row, first, blocks):
    spread = jnp.broadcast_to(index_row, (LANE, W)).T
    lane = lax.broadcasted_iota(jnp.int32, (W, LANE), 1) + first
    parts = [(spread == lane + LANE * j).astype(F32).astype(BF16) for j in range(blocks)]
    return jnp.concatenate(parts, axis=1)


def pack_kernel(
    total,
    root_inverse,
    root_rhs,
    panels,
    inverses,
    rhs,
    parents_all,
    groups_all,
    live_all,
    out,
    facts,
    panel,
    inverse,
    parents,
    groups,
    live,
    sems,
):
    node = lax.axis_index("x")
    side = lax.rem(lax.axis_index("y"), 2)
    here = lax.axis_index(ALL)
    pairs = [
        (groups_all, groups),
        (parents_all, parents),
        (live_all, live),
        (panels.at[node], panel),
        (inverses.at[node], inverse),
        (root_inverse, out.at[:, :W]),
        (root_rhs, out.at[:, W : W + K]),
        (rhs.at[node], out.at[:, W + K : W + 2 * K]),
    ]
    copies = [pltpu.make_async_copy(a, b, sems.at[i]) for i, (a, b) in enumerate(pairs)]
    for copy in copies:
        copy.start()
    for copy in copies:
        copy.wait()
    values = []
    for n in range(2):
        group = groups[n]
        block = lax.rem(group // 2 - here + total + HOP, total) - HOP + lax.rem(here, 2)
        values += [parents[2 * here + n], parents[group], block, lax.rem(group, 2), live[n]]
    place = lax.broadcasted_iota(jnp.int32, facts.shape, 1)
    row = jnp.zeros(facts.shape, jnp.int32)
    for i, value in enumerate(values):
        row = jnp.where(place == i, value, row)
    facts[...] = row

    def half(array):
        return jnp.where(side == 0, array[:, :HALF], array[:, HALF:])

    inverse_half = half(inverse[...])
    out[:, W + 2 * K :] = jnp.concatenate(
        [inverse_half[:, :LANE], half(panel[...]), inverse_half[:, LANE:]], axis=1
    )


def upper_kernel(got, mid_rows, panels, inverses, root, part):
    del panels, inverses
    side = lax.rem(lax.axis_index("y"), 2)
    core = lax.axis_index("c")
    mid_index = mid_rows[pl.ds(lax.axis_index("x"), 1), :]
    solved = dot(got[:, :W], got[:, W : W + K]).astype(BF16)
    root[...] = solved
    spread = dot(got[:, W + 2 * K + LANE :].T, one_hot(mid_index, 0, W // LANE)).astype(BF16)
    products = dot(spread, solved)
    first = pl.multiple_of(side * HALF, 64)
    rhs = got[pl.ds(first, HALF), W + K : W + 2 * K].astype(F32)
    update = (rhs - products[:HALF]).astype(BF16)
    head = update[:LANE]
    tail = jnp.concatenate([jnp.zeros((LANE // 2, K), BF16), update[LANE:]], axis=0)
    rows = pl.ds(pl.multiple_of(core * HALF, 64), HALF)
    inverse_head = got[rows, W + 2 * K : W + 2 * K + LANE]
    inverse_tail = got[rows, W + 2 * K + 2 * LANE :]
    part[...] = (dot(inverse_head, head) + dot(inverse_tail, tail)).astype(BF16)


def ready_kernel(
    rows, panels, rhs, root, facts, low_rows, low_panels, base, spread, low_base, low_spread
):
    del facts
    for n in range(2):
        index = rows[n : n + 1, :]
        turned = panels[n].T
        picked = dot(one_hot(index, 0, W // LANE), root[...]).astype(BF16)
        base[n] = rhs[n].astype(F32) - dot(turned, picked)
        spread[n] = dot(turned, one_hot(index, W, W // LANE)).astype(BF16)
    for n in range(2):
        index = low_rows[n : n + 1, :]
        turned = low_panels[n].T
        picked = dot(one_hot(index, 0, W // LANE), root[...]).astype(BF16)
        low_base[n] = dot(turned, picked)
        low_spread[n] = dot(turned, one_hot(index, 2 * W, W // LANE)).astype(BF16)


def fact(facts, place):
    lane = lax.broadcasted_iota(jnp.int32, facts.shape, 1)
    return jnp.sum(jnp.where(lane == place, facts[...], 0))


def rows_of(mid, parent):
    return mid[pl.ds(pl.multiple_of(parent * W, W), W), :]


def sub_kernel(facts, mid, base, spread, inverse, out):
    updates = [
        (base[n] - dot(spread[n], rows_of(mid, fact(facts, 5 * n)))).astype(BF16) for n in range(2)
    ]
    for n in range(2):
        out[n] = dot(inverse[n], updates[n]).astype(BF16)


def leaf_middle_kernel(
    facts, rows, panels, rhs, root, mid, solved, from_root, base, root_own, mid_own, out, sem
):
    store = pltpu.make_async_copy(solved, out, sem)
    store.start()
    own_rows = root_own.shape[0]
    first = lax.axis_index(ROWS) * own_rows
    row = lax.broadcasted_iota(jnp.int32, (own_rows, W), 0) + first
    column = lax.broadcasted_iota(jnp.int32, (own_rows, W), 1)
    own = (row == column).astype(F32).astype(BF16)
    root_own[...] = dot(own, root[...]).astype(BF16)
    for s in range(mid_own.shape[0]):
        mid_own[s] = dot(own, mid[s * W : (s + 1) * W, :]).astype(BF16)
    picked = [
        dot(one_hot(rows[n : n + 1, :], W, W // LANE), rows_of(mid, fact(facts, 5 * n + 1))).astype(BF16)
        for n in range(2)
    ]
    for n in range(2):
        base[n] = rhs[n].astype(F32) - from_root[n] - dot(panels[n].T, picked[n])
    store.wait()


def leaf_kernel(facts, base, spread, inverse, chip, nearby, outer, out, held, done, sems):
    numbers = [[fact(facts, 5 * n + i) for i in (2, 3, 4)] for n in range(2)]
    for n in range(2):
        block, member, _ = numbers[n]

        @pl.when(jnp.logical_or(block == 0, block == 1))
        def _():
            held[n] = chip[2 * block + member]

        @pl.when(jnp.logical_or(block == -1, block == 2))
        def _():
            held[n] = nearby[jnp.where(block == 2, 2, 0) + member]

        @pl.when(jnp.logical_or(block == -2, block == 3))
        def _():
            held[n] = outer[member]

    row = lax.broadcasted_iota(jnp.int32, (W, K), 0)
    updates = [(base[n] - dot(spread[n], held[n])).astype(BF16) for n in range(2)]
    stores = []
    for n in range(2):
        solved = dot(inverse[n], updates[n])
        done[n] = jnp.where(row < numbers[n][2], solved, 0.0).astype(BF16)
        stores.append(pltpu.make_async_copy(done.at[n], out.at[n], sems.at[n]))
        stores[n].start()
    for store in stores:
        store.wait()


def per_device(
    root_inverse,
    root_rhs,
    mid_panels,
    mid_rows,
    mid_inverse,
    mid_rhs,
    parent_list,
    sub_panels,
    sub_rows,
    sub_inverse,
    sub_rhs,
    group_of,
    leaf_panels,
    leaf_rows,
    leaf_inverse,
    leaf_rhs,
    live_cols,
):
    own_rows = root_inverse.shape[0]
    total = lax.axis_size(ALL)
    parents = parent_list.reshape(-1)
    packed, facts = call(
        functools.partial(pack_kernel, total),
        (shape(own_rows, 1280), shape(1, LANE, dtype=jnp.int32)),
        [HBM] * 8,
        0,
        4 * own_rows * 1280,
        scratch=[pltpu.VMEM((own_rows, W), BF16)] * 2
        + [pltpu.SMEM(a.shape, jnp.int32) for a in (parents, group_of, live_cols)]
        + [pltpu.SemaphoreType.DMA((8,))],
        grant=60,
    )(root_inverse, root_rhs, mid_panels, mid_inverse, mid_rhs, parents, group_of, live_cols)
    got = lax.all_gather(packed, ROWS, axis=0, tiled=True)
    square, tall = shape(2, W, W), shape(2, W, K, dtype=F32)
    thin = shape(2, W, K)
    root, part = call(
        upper_kernel,
        (shape(W, K), shape(HALF, K)),
        [VMEM] * 4,
        2 * W * W * K,
        2 * W * 1280,
    )(got, mid_rows, leaf_panels, leaf_inverse)
    other = lax.ppermute(part, "y", [(i, i ^ 1) for i in range(lax.axis_size("y"))])
    base, spread, from_root, leaf_spread = call(
        ready_kernel,
        (tall, square, tall, square),
        [VMEM] * 7,
        16 * W * W * K,
        16 * W * W + 40 * W * K,
    )(sub_rows, sub_panels, sub_rhs, root, facts, leaf_rows, leaf_panels)
    mid_half = (part.astype(F32) + other.astype(F32)).astype(BF16)
    mid_half, base = lax.optimization_barrier((mid_half, base))
    mid = lax.all_gather(mid_half, ("x", "c"), axis=0, tiled=True)
    solved = call(
        sub_kernel,
        shape(2, W, K),
        [VMEM] * 5,
        4 * W * W * K,
        12 * W * W + 16 * W * K,
    )(facts, mid, base, spread, sub_inverse)
    chips = total // 2
    cross = [((2 * m - 1) % total, 2 * m) for m in range(chips)]
    cross += [((2 * m + 2) % total, 2 * m + 1) for m in range(chips)]
    straight = [((2 * m - 2) % total, 2 * m) for m in range(chips)]
    straight += [((2 * m + 3) % total, 2 * m + 1) for m in range(chips)]
    inner = lax.ppermute(solved, ALL, cross)
    outer = lax.ppermute(solved, ALL, straight)
    chip = lax.all_gather(solved, "c", axis=0, tiled=True)
    leaf_base, root_own, mid_own, sub_solution = call(
        leaf_middle_kernel,
        (tall, shape(own_rows, K), shape(mid_rows.shape[0], own_rows, K), thin),
        [VMEM] * 8,
        4 * W * W * K,
        8 * W * W + 24 * W * K,
        places=(VMEM,) * 3 + (HBM,),
        scratch=[pltpu.SemaphoreType.DMA],
    )(facts, leaf_rows, leaf_panels, leaf_rhs, root, mid, solved, from_root)
    inner, chip, leaf_base = lax.optimization_barrier((inner, chip, leaf_base))
    nearby = lax.all_gather(inner, "c", axis=0, tiled=True)
    leaf_solution = call(
        leaf_kernel,
        shape(2, W, K),
        [VMEM] * 7,
        4 * W * W * K,
        12 * W * W + 24 * W * K,
        places=HBM,
        scratch=[pltpu.VMEM((2, W, K), BF16)] * 2 + [pltpu.SemaphoreType.DMA((2,))],
    )(facts, leaf_base, leaf_spread, leaf_inverse, chip, nearby, outer)
    return (root_own, mid_own, sub_solution, leaf_solution)


def solution(mesh):
    chips = Mesh(mesh.devices.reshape(8, 4, 8, 2), ALL)
    lower = P(ALL, None, None)
    return jax.shard_map(
        per_device,
        mesh=chips,
        in_specs=(
            P(ROWS, None),
            P(ROWS, None),
            P(None, ROWS, None),
            P(),
            P(None, ROWS, None),
            P(None, ROWS, None),
            P(),
            lower,
            P(ALL, None),
            lower,
            lower,
            P(ALL),
            lower,
            P(ALL, None),
            lower,
            lower,
            P(ALL),
        ),
        out_specs=(P(ROWS, None), P(None, ROWS, None), lower, lower),
        check_vma=False,
    )
```
